512 devices in a mesh: tm: 64 (over x_hi, z, core), height: 8 (over y, x_lo).
Axes of the slice: x: 4 (x_hi: 2, x_lo: 2; x = x_hi * 2 + x_lo), y: 4, z: 16, core: 2. Of those that a mesh axis runs over, the one named last changes fastest.
Arguments:
- queries: bfloat16 [384, 32, 6, 1536], P('tm', 'height'), may hold values from -6 to 6
- keys: bfloat16 [384, 32, 6, 1536], P('tm', 'height'), may hold values from -6 to 6
- values: bfloat16 [384, 32, 6, 1536], P('tm', 'height'), may hold values from -6 to 6
- grad_out: bfloat16 [384, 32, 6, 1536], P('tm', 'height'), may hold values from -6 to 6
- reach: int32 [2, 12], replicated, may hold values from 0 to 1, as said below
Outputs:
- attn_out: bfloat16 [384, 32, 6, 1536], P('tm', 'height')
- grad_queries: bfloat16 [384, 32, 6, 1536], P('tm', 'height')
- grad_keys: bfloat16 [384, 32, 6, 1536], P('tm', 'height')
- grad_values: bfloat16 [384, 32, 6, 1536], P('tm', 'height')
The draws below stay inside these ranges and needn't reach their ends.
Inputs may be any that keep to these rules, and one draw needn't show every extreme that they name: `reach`: in each row exactly half of the 12 heads have 1.
All inputs are finite; a program needn't handle non-finite values.
Results may differ from the reference program's by a relative error of at most 0.024.
Values may be sent and summed in bfloat16 or wider, within the bound.
A program may use at most 128 MiB of HBM per device.

```python
import jax
import jax.numpy as jnp
from jax import lax

HEADS = 12
HEAD_DIM = 128
TILE_T = 6
TILE_H = 8
COLS = 6
CLIP_TILES = 64
FRAMES = 384
ROWS = 32


def draw_queries(key, part):
    key = jax.random.fold_in(key, 11)
    full_shape = (FRAMES, ROWS, COLS, HEADS * HEAD_DIM)
    return jnp.clip(jax.random.normal(key, full_shape, jnp.float32), -6.0, 6.0).astype(jnp.bfloat16)


def draw_keys(key, part):
    key = jax.random.fold_in(key, 23)
    full_shape = (FRAMES, ROWS, COLS, HEADS * HEAD_DIM)
    return jnp.clip(jax.random.normal(key, full_shape, jnp.float32), -6.0, 6.0).astype(jnp.bfloat16)


def draw_reach(key, part):
    key = jax.random.fold_in(key, 37)
    first_key, second_key = jax.random.split(key)
    backward = jax.random.permutation(first_key, HEADS) % 2
    forward = jax.random.permutation(second_key, HEADS) % 2
    return jnp.stack([backward, forward]).astype(jnp.int32)


def block_scale(stream_key, extent, pieces, least, largest):
    loudness = 1.0
    for axis_at, parts in pieces:
        steps = jax.random.uniform(jax.random.fold_in(jax.random.fold_in(stream_key, 6), axis_at), (parts,), jnp.float32, least / len(pieces), largest / len(pieces))
        loudness = loudness * jnp.repeat(jnp.exp(steps), extent[axis_at] // parts).reshape((-1,) + (1,) * (len(extent) - 1 - axis_at))
    return loudness


def centred(key, dims, scale, most, pieces=(), kind=jnp.bfloat16):
    entries = scale * jax.random.normal(key, dims, jnp.float32)
    if pieces:
        entries = entries * block_scale(key, dims, pieces, -0.22, 0.18)
    return jnp.clip(entries, -most, most).astype(kind)


def setup_inputs(seed: int = 0) -> dict:
    arg_keys = jax.random.split(jax.random.key(seed), 6)
    queries = draw_queries(jax.random.fold_in(arg_keys[5], 71), 0)
    keys = draw_keys(jax.random.fold_in(arg_keys[5], 71), 0)
    values = centred(arg_keys[2], (FRAMES, ROWS, COLS, HEADS * HEAD_DIM), 1.0, 6.0, ((0, 64), (1, 8)))
    grad_out = centred(arg_keys[3], (FRAMES, ROWS, COLS, HEADS * HEAD_DIM), 1.0, 6.0, ((0, 64), (1, 8)))
    reach = draw_reach(jax.random.fold_in(arg_keys[5], 71), 0)
    return {"queries": queries, "keys": keys, "values": values, "grad_out": grad_out, "reach": reach}


def to_tiles(array):
    tile_count = array.shape[0] // TILE_T
    band_count = array.shape[1] // TILE_H
    half_rows = TILE_H // 2
    shaped = array.reshape(tile_count, TILE_T, band_count, 2, half_rows, COLS, HEADS, HEAD_DIM)
    shaped = shaped.transpose(0, 2, 3, 1, 4, 5, 6, 7)
    return shaped.reshape(tile_count, band_count, 2 * TILE_T * half_rows * COLS, HEADS, HEAD_DIM)


def from_tiles(tiled):
    tile_count = tiled.shape[0]
    band_count = tiled.shape[1]
    half_rows = TILE_H // 2
    shaped = tiled.reshape(tile_count, band_count, 2, TILE_T, half_rows, COLS, HEADS, HEAD_DIM)
    shaped = shaped.transpose(0, 3, 1, 2, 4, 5, 6, 7)
    return shaped.reshape(tile_count * TILE_T, band_count * TILE_H, COLS, HEADS * HEAD_DIM)


def rounded(array):
    return lax.optimization_barrier(array.astype(jnp.bfloat16)).astype(jnp.float32)


def reference(queries, keys, values, grad_out, reach):
    factor = HEAD_DIM ** -0.5
    query_tiles = to_tiles(queries)
    grad_tiles = to_tiles(grad_out)
    key_tiles = to_tiles(keys)
    value_tiles = to_tiles(values)
    tile_count = query_tiles.shape[0]
    band_count = query_tiles.shape[1]
    tile_tokens = query_tiles.shape[2]
    half_tokens = tile_tokens // 2
    blank = jnp.zeros_like(key_tiles[:1])
    key_padded = jnp.concatenate([blank, key_tiles, blank], axis=0)
    value_padded = jnp.concatenate([blank, value_tiles, blank], axis=0)
    offsets = jnp.arange(3, dtype=jnp.int32) - 1

    def window(padded, tile_index):
        block = lax.dynamic_slice_in_dim(padded, tile_index, 3, 0)
        block = block.transpose(1, 0, 2, 3, 4)
        return block.reshape(band_count, 3 * tile_tokens, HEADS, HEAD_DIM).astype(jnp.float32)

    def step(carry, tile_index):
        prev_keys, prev_values, curr_keys, curr_values = carry
        query_tile = lax.dynamic_index_in_dim(query_tiles, tile_index, 0, keepdims=False).astype(jnp.float32)
        grad_tile = lax.dynamic_index_in_dim(grad_tiles, tile_index, 0, keepdims=False).astype(jnp.float32)
        key_window = window(key_padded, tile_index)
        value_window = window(value_padded, tile_index)
        allowed = (offsets[None, :] >= -reach[0][:, None]) & (offsets[None, :] <= reach[1][:, None])
        clip_pos = tile_index % CLIP_TILES
        inside = (clip_pos + offsets >= 0) & (clip_pos + offsets < CLIP_TILES)
        allowed = allowed & inside[None, :]
        key_mask = jnp.broadcast_to(allowed[:, :, None], (HEADS, 3, tile_tokens)).reshape(HEADS, 3 * tile_tokens)
        key_mask = key_mask[None, :, None, :]
        scores = jnp.einsum("nqhd,nkhd->nhqk", query_tile, key_window) * factor
        masked = jnp.where(key_mask, scores, -1e30)
        row_max = jnp.max(masked, axis=-1)
        log_total = row_max + jnp.log(jnp.sum(jnp.exp(masked - row_max[..., None]), axis=-1))
        probability = jnp.where(key_mask, jnp.exp(scores - log_total[..., None]), 0.0)
        weights = rounded(probability)
        attended = jnp.einsum("nhqk,nkhd->nqhd", weights, value_window).astype(jnp.bfloat16)
        row_dot = jnp.einsum("nqhd,nqhd->nhq", grad_tile, attended.astype(jnp.float32))
        grad_prob = jnp.einsum("nqhd,nkhd->nhqk", grad_tile, value_window)
        grad_score = rounded(probability * (grad_prob - row_dot[..., None]))
        grad_query = (jnp.einsum("nhqk,nkhd->nqhd", grad_score, key_window) * factor).astype(jnp.bfloat16)
        split_score = grad_score.reshape(band_count, HEADS, 2, half_tokens, 3 * tile_tokens)
        split_weight = weights.reshape(band_count, HEADS, 2, half_tokens, 3 * tile_tokens)
        split_query = query_tile.reshape(band_count, 2, half_tokens, HEADS, HEAD_DIM)
        split_grad = grad_tile.reshape(band_count, 2, half_tokens, HEADS, HEAD_DIM)
        key_parts = rounded(jnp.einsum("nhsqk,nsqhd->nskhd", split_score, split_query) * factor)
        value_parts = rounded(jnp.einsum("nhsqk,nsqhd->nskhd", split_weight, split_grad))
        key_sum = jnp.sum(key_parts, axis=1).reshape(band_count, 3, tile_tokens, HEADS, HEAD_DIM)
        value_sum = jnp.sum(value_parts, axis=1).reshape(band_count, 3, tile_tokens, HEADS, HEAD_DIM)
        done_keys = prev_keys + key_sum[:, 0]
        done_values = prev_values + value_sum[:, 0]
        carry = (curr_keys + key_sum[:, 1], curr_values + value_sum[:, 1], key_sum[:, 2], value_sum[:, 2])
        return carry, (attended, grad_query, done_keys.astype(jnp.bfloat16), done_values.astype(jnp.bfloat16))

    zeros = jnp.zeros((band_count, tile_tokens, HEADS, HEAD_DIM), jnp.float32)
    final, stacked = lax.scan(step, (zeros, zeros, zeros, zeros), jnp.arange(tile_count, dtype=jnp.int32))
    attended, grad_query, done_keys, done_values = stacked
    grad_keys = jnp.concatenate([done_keys[1:], final[0].astype(jnp.bfloat16)[None]], axis=0)
    grad_values = jnp.concatenate([done_values[1:], final[1].astype(jnp.bfloat16)[None]], axis=0)
    return (from_tiles(attended), from_tiles(grad_query), from_tiles(grad_keys), from_tiles(grad_values))
```

```python
import functools
import math

import jax
import jax.numpy as jnp
from jax import lax
from jax.experimental import pallas as pl
from jax.experimental.pallas import tpu as pltpu
from jax.sharding import PartitionSpec as P

MESH = pl.DeviceIdType.MESH
HEADS, SIZE = 12, 128
FRAMES, ROWS, COLS = 6, 4, 6
OWN = HEADS // 2
HALF = (FRAMES, COLS, ROWS, SIZE)
TOKENS = 2 * FRAMES * COLS * ROWS
FACTOR = SIZE**-0.5
FACTOR2 = FACTOR * math.log2(math.e)
RING = 32


def dot(a, b, over_a, over_b):
    return lax.dot_general(
        a, b, (((over_a,), (over_b,)), ((), ())), preferred_element_type=jnp.float32
    )


def one_head(q, d, ks, vs, biases):
    scores = [dot(q, k, 1, 1) for k in ks]
    scores = [s if b is None else s + b for s, b in zip(scores, biases)]
    top = functools.reduce(jnp.maximum, [jnp.max(s, axis=1, keepdims=True) for s in scores])
    raised = [jnp.exp2((s - top) * FACTOR2) for s in scores]
    total = sum(jnp.sum(e, axis=1, keepdims=True) for e in raised)
    inverse = 1.0 / total
    probability = [e * inverse for e in raised]
    weights = [p.astype(jnp.bfloat16) for p in probability]
    attended = sum(dot(w, v, 1, 0) for w, v in zip(weights, vs)).astype(jnp.bfloat16)
    row_dot = jnp.sum(
        attended.astype(jnp.float32) * d.astype(jnp.float32), axis=1, keepdims=True
    )
    grad_prob = [dot(d, v, 1, 1) for v in vs]
    grad_score = [
        (p * (g - row_dot)).astype(jnp.bfloat16) for p, g in zip(probability, grad_prob)
    ]
    grad_query = sum(dot(s, k, 1, 0) for s, k in zip(grad_score, ks)) * FACTOR
    key_parts = [dot(s, q, 0, 0) * FACTOR for s in grad_score]
    value_parts = [dot(w, d, 0, 0) for w in weights]
    return attended, grad_query.astype(jnp.bfloat16), key_parts, value_parts


def kernel(
    reach, k_in, v_in, q_in, d_in, o_out, dq_out, dk_out, dv_out,
    tile, near, local_grad, sent, got, done,
    own_sem, xs_sem, xr_sem, ks_sem, kr_sem, gs_sem, gr_sem, os_sem, or_sem, ol_sem,
):
    tm, height = lax.axis_index("tm"), lax.axis_index("height")
    count = lax.axis_size("tm")
    inputs = (k_in, v_in, q_in, d_in)
    outputs = (o_out, dq_out, dk_out, dv_out)
    other = height + 1 - 2 * (height % 2)
    partner = (tm, other)
    flip_next = (tm % RING + 1) // RING
    flip_prev = 1 - (tm % RING + RING - 1) // RING
    following = ((tm + 1) % count, height + flip_next * (other - height))
    preceding = ((tm + count - 1) % count, height + flip_prev * (other - height))
    side = (height % 2 + tm // RING) % 2
    mine, theirs = side * OWN, (1 - side) * OWN

    def own_copy(j, a):
        return pltpu.make_async_copy(
            inputs[a].at[:, :, mine + j], tile.at[j, a, 0], own_sem.at[j, a]
        )

    def remote(src, dst, send, recv, device):
        return pltpu.make_async_remote_copy(
            src_ref=src, dst_ref=dst, send_sem=send, recv_sem=recv, device_id=device,
            device_id_type=MESH,
        )

    def half_copy(j, a):
        return remote(
            inputs[a].at[:, :, theirs + j], tile.at[j, a, 1], xs_sem.at[j, a], xr_sem.at[j, a], partner
        )

    def key_copies(j):
        block = tile.at[j, pl.ds(0, 2)]
        return (
            remote(block, near.at[j, 0], ks_sem.at[j, 0], kr_sem.at[j, 0], following),
            remote(block, near.at[j, 1], ks_sem.at[j, 1], kr_sem.at[j, 1], preceding),
        )

    def grad_copies(j):
        return (
            remote(sent.at[j, 1], got.at[j, 0], gs_sem.at[j, 0], gr_sem.at[j, 0], following),
            remote(sent.at[j, 0], got.at[j, 1], gs_sem.at[j, 1], gr_sem.at[j, 1], preceding),
        )

    def out_own(j, a):
        return pltpu.make_async_copy(
            done.at[j, a, 0], outputs[a].at[:, :, mine + j], ol_sem.at[j, a]
        )

    def out_half(j, a):
        return remote(
            done.at[j, a, 1], outputs[a].at[:, :, mine + j], os_sem.at[j, a], or_sem.at[j, a], partner
        )

    def out_half_in(j, a):
        return remote(
            done.at[j, a, 1], outputs[a].at[:, :, theirs + j], os_sem.at[j, a], or_sem.at[j, a], partner
        )

    barrier = pltpu.get_barrier_semaphore()
    for device in (partner, following, preceding):
        pl.semaphore_signal(barrier, inc=1, device_id=device, device_id_type=MESH)
    pl.semaphore_wait(barrier, 3)

    def begin(j, carry):
        for a in range(4):
            half_copy(j, a).start()
        for a in range(4):
            own_copy(j, a).start()
        return carry

    lax.fori_loop(0, OWN, begin, 0)

    def flat(x):
        return x.reshape(TOKENS, SIZE)

    def tiled(x):
        return x.astype(jnp.bfloat16).reshape((2,) + HALF)

    def step(it, carry):
        @pl.when(it < OWN)
        def _():
            j = it
            for a in range(4):
                own_copy(j, a).wait()
                half_copy(j, a).wait_recv()
            for copy in key_copies(j):
                copy.start()

        @pl.when((it >= 1) & (it < OWN + 1))
        def _():
            j = it - 1
            for copy in key_copies(j):
                copy.wait_recv()
            k, v, q, d = [flat(tile[j, a]) for a in range(4)]
            ks = [k, flat(near[j, 0, 0]), flat(near[j, 1, 0])]
            vs = [v, flat(near[j, 0, 1]), flat(near[j, 1, 1])]
            back = (reach[0, mine + j] >= 1) & (tm >= 1)
            ahead = (reach[1, mine + j] >= 1) & (tm < count - 1)
            biases = [None, jnp.where(back, 0.0, -1e30), jnp.where(ahead, 0.0, -1e30)]
            attended, grad_query, key_parts, value_parts = one_head(q, d, ks, vs, biases)
            done[j, 0] = tiled(attended)
            done[j, 1] = tiled(grad_query)
            local_grad[j % 2, 0] = key_parts[0]
            local_grad[j % 2, 1] = value_parts[0]
            for way in range(2):
                sent[j, way, 0] = tiled(key_parts[1 + way])
                sent[j, way, 1] = tiled(value_parts[1 + way])
            for copy in grad_copies(j):
                copy.start()
            for a in range(2):
                out_half(j, a).start()
                out_own(j, a).start()

        @pl.when(it >= 2)
        def _():
            j = it - 2
            for copy in grad_copies(j):
                copy.wait_recv()
            for part in range(2):
                total = local_grad[j % 2, part]
                for way in range(2):
                    total = total + flat(got[j, way, part]).astype(jnp.float32)
                done[j, 2 + part] = tiled(total)
            for a in range(2, 4):
                out_half(j, a).start()
                out_own(j, a).start()

        return carry

    lax.fori_loop(0, OWN + 2, step, 0)

    def finish(j, carry):
        for a in range(4):
            half_copy(j, a).wait_send()
            out_own(j, a).wait()
            out_half(j, a).wait_send()
            out_half_in(j, a).wait_recv()
        for copy in key_copies(j) + grad_copies(j):
            copy.wait_send()
        return carry

    lax.fori_loop(0, OWN, finish, 0)


def local(queries, keys, values, grad_out, reach):
    def split(x):
        return x.reshape(FRAMES, ROWS, COLS, HEADS, SIZE).transpose(0, 2, 3, 1, 4)

    def join(x):
        return x.transpose(0, 3, 1, 2, 4).reshape(FRAMES, ROWS, COLS, HEADS * SIZE)

    shape = (FRAMES, COLS, HEADS, ROWS, SIZE)
    anywhere = pl.BlockSpec(memory_space=pl.ANY)
    sems = pltpu.SemaphoreType.DMA
    outs = pl.pallas_call(
        kernel,
        out_shape=[jax.ShapeDtypeStruct(shape, jnp.bfloat16)] * 4,
        in_specs=[pl.BlockSpec(memory_space=pltpu.SMEM)] + [anywhere] * 4,
        out_specs=[anywhere] * 4,
        scratch_shapes=[
            pltpu.VMEM((OWN, 4, 2) + HALF, jnp.bfloat16),
            pltpu.VMEM((OWN, 2, 2, 2) + HALF, jnp.bfloat16),
            pltpu.VMEM((2, 2, TOKENS, SIZE), jnp.float32),
            pltpu.VMEM((OWN, 2, 2, 2) + HALF, jnp.bfloat16),
            pltpu.VMEM((OWN, 2, 2, 2) + HALF, jnp.bfloat16),
            pltpu.VMEM((OWN, 4, 2) + HALF, jnp.bfloat16),
            sems((OWN, 4)), sems((OWN, 4)), sems((OWN, 4)),
            sems((OWN, 2)), sems((OWN, 2)), sems((OWN, 2)), sems((OWN, 2)),
            sems((OWN, 4)), sems((OWN, 4)), sems((OWN, 4)),
        ],
        compiler_params=pltpu.CompilerParams(
            collective_id=0, has_side_effects=True, vmem_limit_bytes=56 << 20
        ),
    )(reach, split(keys), split(values), split(queries), split(grad_out))
    return tuple(join(x) for x in outs)


def solution(mesh):
    spec = P("tm", "height", None, None)
    return jax.shard_map(
        local,
        mesh=mesh,
        in_specs=(spec, spec, spec, spec, P()),
        out_specs=(spec, spec, spec, spec),
        check_vma=False,
    )
```

```python
import functools
import math

import jax
import jax.numpy as jnp
from jax import lax
from jax.experimental import pallas as pl
from jax.experimental.pallas import tpu as pltpu
from jax.sharding import PartitionSpec as P

MESH = pl.DeviceIdType.MESH
HEADS, SIZE = 12, 128
FRAMES, ROWS, COLS = 6, 4, 6
OWN = HEADS // 2
HALF = (FRAMES, COLS, ROWS, SIZE)
TOKENS = 2 * FRAMES * COLS * ROWS
FACTOR = SIZE**-0.5
FACTOR2 = FACTOR * math.log2(math.e)
RING = 32


def dot(a, b, over_a, over_b):
    return lax.dot_general(
        a, b, (((over_a,), (over_b,)), ((), ())), preferred_element_type=jnp.float32
    )


def one_head(q, d, ks, vs, biases):
    scores = [dot(q, k, 1, 1) for k in ks]
    scores = [s if b is None else s + b for s, b in zip(scores, biases)]
    top = functools.reduce(jnp.maximum, [jnp.max(s, axis=1, keepdims=True) for s in scores])
    raised = [jnp.exp2((s - top) * FACTOR2) for s in scores]
    total = sum(jnp.sum(e, axis=1, keepdims=True) for e in raised)
    inverse = 1.0 / total
    probability = [e * inverse for e in raised]
    weights = [p.astype(jnp.bfloat16) for p in probability]
    attended = sum(dot(w, v, 1, 0) for w, v in zip(weights, vs)).astype(jnp.bfloat16)
    row_dot = jnp.sum(
        attended.astype(jnp.float32) * d.astype(jnp.float32), axis=1, keepdims=True
    )
    grad_prob = [dot(d, v, 1, 1) for v in vs]
    grad_score = [
        (p * (g - row_dot)).astype(jnp.bfloat16) for p, g in zip(probability, grad_prob)
    ]
    grad_query = sum(dot(s, k, 1, 0) for s, k in zip(grad_score, ks)) * FACTOR
    key_parts = [dot(s, q, 0, 0) * FACTOR for s in grad_score]
    value_parts = [dot(w, d, 0, 0) for w in weights]
    return attended, grad_query.astype(jnp.bfloat16), key_parts, value_parts


def kernel(
    reach, k_in, v_in, q_in, d_in, o_out, dq_out, dk_out, dv_out,
    tile, near, local_grad, sent, got, done,
    own_sem, xs_sem, xr_sem, ks_sem, kr_sem, gs_sem, gr_sem, os_sem, or_sem, ol_sem, hello,
):
    tm, height = lax.axis_index("tm"), lax.axis_index("height")
    count = lax.axis_size("tm")
    inputs = (k_in, v_in, q_in, d_in)
    outputs = (o_out, dq_out, dk_out, dv_out)
    other = height + 1 - 2 * (height % 2)
    partner = (tm, other)
    flip_next = (tm % RING + 1) // RING
    flip_prev = 1 - (tm % RING + RING - 1) // RING
    following = ((tm + 1) % count, height + flip_next * (other - height))
    preceding = ((tm + count - 1) % count, height + flip_prev * (other - height))
    side = (height % 2 + tm // RING) % 2
    mine, theirs = side * OWN, (1 - side) * OWN

    def own_copy(j, a):
        return pltpu.make_async_copy(
            inputs[a].at[:, :, mine + j], tile.at[j, a, 0], own_sem.at[j, a]
        )

    def remote(src, dst, send, recv, device):
        return pltpu.make_async_remote_copy(
            src_ref=src, dst_ref=dst, send_sem=send, recv_sem=recv, device_id=device,
            device_id_type=MESH,
        )

    def half_copy(j, a):
        return remote(
            inputs[a].at[:, :, theirs + j], tile.at[j, a, 1], xs_sem.at[j, a], xr_sem.at[j, a], partner
        )

    def key_copies(j):
        block = tile.at[j, pl.ds(0, 2)]
        return (
            remote(block, near.at[j, 0], ks_sem.at[j, 0], kr_sem.at[j, 0], following),
            remote(block, near.at[j, 1], ks_sem.at[j, 1], kr_sem.at[j, 1], preceding),
        )

    def grad_copies(j):
        return (
            remote(sent.at[j, 1], got.at[j, 0], gs_sem.at[j, 0], gr_sem.at[j, 0], following),
            remote(sent.at[j, 0], got.at[j, 1], gs_sem.at[j, 1], gr_sem.at[j, 1], preceding),
        )

    def out_own(j, a):
        return pltpu.make_async_copy(
            done.at[j, a, 0], outputs[a].at[:, :, mine + j], ol_sem.at[j, a]
        )

    def out_half(j, a):
        return remote(
            done.at[j, a, 1], outputs[a].at[:, :, mine + j], os_sem.at[j, a], or_sem.at[j, a], partner
        )

    def out_half_in(j, a):
        return remote(
            done.at[j, a, 1], outputs[a].at[:, :, theirs + j], os_sem.at[j, a], or_sem.at[j, a], partner
        )

    odd = tm % 2
    seam = (1 - odd) * flip_prev + odd * flip_next
    barrier = pltpu.get_barrier_semaphore()
    pl.semaphore_signal(barrier, inc=1, device_id=partner, device_id_type=MESH)

    @pl.when(odd == 1)
    def _():
        pl.semaphore_signal(barrier, inc=1, device_id=preceding, device_id_type=MESH)

    @pl.when((odd == 1) & (seam == 0))
    def _():
        pl.semaphore_signal(barrier, inc=1, device_id=following, device_id_type=MESH)

    @pl.when((odd == 0) & (seam == 1))
    def _():
        pl.semaphore_signal(barrier, inc=1, device_id=preceding, device_id_type=MESH)

    pl.semaphore_wait(barrier, 3 - 2 * odd + (2 * odd - 1) * seam)

    for first in (0, 2):

        def begin(j, carry, first=first):
            for a in (first, first + 1):
                half_copy(j, a).start()
            for a in (first, first + 1):
                own_copy(j, a).start()
            return carry

        lax.fori_loop(0, OWN, begin, 0)

    @pl.when(odd == 0)
    def _():
        pl.semaphore_signal(hello.at[0], inc=1, device_id=following, device_id_type=MESH)

    @pl.when((odd == 0) & (seam == 0))
    def _():
        pl.semaphore_signal(hello.at[1], inc=1, device_id=preceding, device_id_type=MESH)

    @pl.when((odd == 1) & (seam == 1))
    def _():
        pl.semaphore_signal(hello.at[1], inc=1, device_id=following, device_id_type=MESH)

    @pl.when(odd == 1)
    def _():
        pl.semaphore_wait(hello.at[0], 1)

    @pl.when(odd != seam)
    def _():
        pl.semaphore_wait(hello.at[1], 1)

    def flat(x):
        return x.reshape(TOKENS, SIZE)

    def tiled(x):
        return x.astype(jnp.bfloat16).reshape((2,) + HALF)

    def arrived(j, first):
        for a in (first, first + 1):
            own_copy(j, a).wait()
            half_copy(j, a).wait_recv()

    def forward(j, carry):
        arrived(j, 0)
        for copy in key_copies(j):
            copy.start()
        return carry

    lax.fori_loop(0, OWN, forward, 0)

    def compute(j, carry):
        arrived(j, 2)
        for copy in key_copies(j):
            copy.wait_recv()
        k, v, q, d = [flat(tile[j, a]) for a in range(4)]
        ks = [k, flat(near[j, 0, 0]), flat(near[j, 1, 0])]
        vs = [v, flat(near[j, 0, 1]), flat(near[j, 1, 1])]
        back = (reach[0, mine + j] >= 1) & (tm >= 1)
        ahead = (reach[1, mine + j] >= 1) & (tm < count - 1)
        biases = [None, jnp.where(back, 0.0, -1e30), jnp.where(ahead, 0.0, -1e30)]
        attended, grad_query, key_parts, value_parts = one_head(q, d, ks, vs, biases)
        for way in range(2):
            sent[j, way, 0] = tiled(key_parts[1 + way])
            sent[j, way, 1] = tiled(value_parts[1 + way])
        for copy in grad_copies(j):
            copy.start()
        done[j, 0] = tiled(attended)
        done[j, 1] = tiled(grad_query)
        for a in range(2):
            out_half(j, a).start()
            out_own(j, a).start()
        local_grad[j, 0] = key_parts[0]
        local_grad[j, 1] = value_parts[0]
        return carry

    lax.fori_loop(0, OWN, compute, 0)

    def gather(j, carry):
        for copy in grad_copies(j):
            copy.wait_recv()
        for part in range(2):
            total = local_grad[j, part]
            for way in range(2):
                total = total + flat(got[j, way, part]).astype(jnp.float32)
            done[j, 2 + part] = tiled(total)
            out_half(j, 2 + part).start()
            out_own(j, 2 + part).start()
        return carry

    lax.fori_loop(0, OWN, gather, 0)

    def finish(j, carry):
        for a in range(4):
            half_copy(j, a).wait_send()
            out_own(j, a).wait()
            out_half(j, a).wait_send()
            out_half_in(j, a).wait_recv()
        for copy in key_copies(j) + grad_copies(j):
            copy.wait_send()
        return carry

    lax.fori_loop(0, OWN, finish, 0)


def local(queries, keys, values, grad_out, reach):
    def split(x):
        return x.reshape(FRAMES, ROWS, COLS, HEADS, SIZE).transpose(0, 2, 3, 1, 4)

    def join(x):
        return x.transpose(0, 3, 1, 2, 4).reshape(FRAMES, ROWS, COLS, HEADS * SIZE)

    shape = (FRAMES, COLS, HEADS, ROWS, SIZE)
    anywhere = pl.BlockSpec(memory_space=pl.ANY)
    sems = pltpu.SemaphoreType.DMA
    outs = pl.pallas_call(
        kernel,
        out_shape=[jax.ShapeDtypeStruct(shape, jnp.bfloat16)] * 4,
        in_specs=[pl.BlockSpec(memory_space=pltpu.SMEM)] + [anywhere] * 4,
        out_specs=[anywhere] * 4,
        scratch_shapes=[
            pltpu.VMEM((OWN, 4, 2) + HALF, jnp.bfloat16),
            pltpu.VMEM((OWN, 2, 2, 2) + HALF, jnp.bfloat16),
            pltpu.VMEM((OWN, 2, TOKENS, SIZE), jnp.float32),
            pltpu.VMEM((OWN, 2, 2, 2) + HALF, jnp.bfloat16),
            pltpu.VMEM((OWN, 2, 2, 2) + HALF, jnp.bfloat16),
            pltpu.VMEM((OWN, 4, 2) + HALF, jnp.bfloat16),
            sems((OWN, 4)), sems((OWN, 4)), sems((OWN, 4)),
            sems((OWN, 2)), sems((OWN, 2)), sems((OWN, 2)), sems((OWN, 2)),
            sems((OWN, 4)), sems((OWN, 4)), sems((OWN, 4)),
            pltpu.SemaphoreType.REGULAR((2,)),
        ],
        compiler_params=pltpu.CompilerParams(
            collective_id=0, has_side_effects=True, vmem_limit_bytes=56 << 20
        ),
    )(reach, split(keys), split(values), split(queries), split(grad_out))
    return tuple(join(x) for x in outs)


def solution(mesh):
    spec = P("tm", "height", None, None)
    return jax.shard_map(
        local,
        mesh=mesh,
        in_specs=(spec, spec, spec, spec, P()),
        out_specs=(spec, spec, spec, spec),
        check_vma=False,
    )
```

```python
import functools
import math

import jax
import jax.numpy as jnp
from jax import lax
from jax.experimental import pallas as pl
from jax.experimental.pallas import tpu as pltpu
from jax.sharding import PartitionSpec as P

MESH = pl.DeviceIdType.MESH
HEADS, SIZE = 12, 128
FRAMES, ROWS, COLS = 6, 4, 6
OWN = HEADS // 2
HALF = (FRAMES, COLS, ROWS, SIZE)
TOKENS = 2 * FRAMES * COLS * ROWS
FACTOR = SIZE**-0.5
FACTOR2 = FACTOR * math.log2(math.e)
RING = 32


def dot(a, b, over_a, over_b):
    return lax.dot_general(
        a, b, (((over_a,), (over_b,)), ((), ())), preferred_element_type=jnp.float32
    )


def one_head(q, d, ks, vs, biases):
    scores = [dot(q, k, 1, 1) for k in ks]
    scores = [s if b is None else s + b for s, b in zip(scores, biases)]
    top = functools.reduce(jnp.maximum, [jnp.max(s, axis=1, keepdims=True) for s in scores])
    raised = [jnp.exp2((s - top) * FACTOR2) for s in scores]
    total = sum(jnp.sum(e, axis=1, keepdims=True) for e in raised)
    inverse = 1.0 / total
    probability = [e * inverse for e in raised]
    weights = [p.astype(jnp.bfloat16) for p in probability]
    attended = sum(dot(w, v, 1, 0) for w, v in zip(weights, vs)).astype(jnp.bfloat16)
    row_dot = jnp.sum(
        attended.astype(jnp.float32) * d.astype(jnp.float32), axis=1, keepdims=True
    )
    grad_prob = [dot(d, v, 1, 1) for v in vs]
    grad_score = [
        (p * (g - row_dot)).astype(jnp.bfloat16) for p, g in zip(probability, grad_prob)
    ]
    grad_query = sum(dot(s, k, 1, 0) for s, k in zip(grad_score, ks)) * FACTOR
    key_parts = [dot(s, q, 0, 0) * FACTOR for s in grad_score]
    value_parts = [dot(w, d, 0, 0) for w in weights]
    return attended, grad_query.astype(jnp.bfloat16), key_parts, value_parts


def kernel(
    reach_in, k_in, v_in, q_in, d_in, o_out, dq_out, dk_out, dv_out,
    reach, tile, near, local_grad, sent, got, done, reach_sem,
    own_sem, xs_sem, xr_sem, ks_sem, kr_sem, gs_sem, gr_sem, os_sem, or_sem, ol_sem, hello,
):
    tm, height = lax.axis_index("tm"), lax.axis_index("height")
    count = lax.axis_size("tm")
    inputs = (k_in, v_in, q_in, d_in)
    outputs = (o_out, dq_out, dk_out, dv_out)
    other = height + 1 - 2 * (height % 2)
    partner = (tm, other)
    flip_next = (tm % RING + 1) // RING
    flip_prev = 1 - (tm % RING + RING - 1) // RING
    following = ((tm + 1) % count, height + flip_next * (other - height))
    preceding = ((tm + count - 1) % count, height + flip_prev * (other - height))
    side = (height % 2 + tm // RING) % 2
    mine, theirs = side * OWN, (1 - side) * OWN

    def own_copy(j, a):
        return pltpu.make_async_copy(
            inputs[a].at[:, :, mine + j], tile.at[j, a, 0], own_sem.at[j, a]
        )

    def remote(src, dst, send, recv, device):
        return pltpu.make_async_remote_copy(
            src_ref=src, dst_ref=dst, send_sem=send, recv_sem=recv, device_id=device,
            device_id_type=MESH,
        )

    def half_copy(j, a):
        return remote(
            inputs[a].at[:, :, theirs + j], tile.at[j, a, 1], xs_sem.at[j, a], xr_sem.at[j, a], partner
        )

    def key_copies(j):
        block = tile.at[j, pl.ds(0, 2)]
        return (
            remote(block, near.at[j, 0], ks_sem.at[j, 0], kr_sem.at[j, 0], following),
            remote(block, near.at[j, 1], ks_sem.at[j, 1], kr_sem.at[j, 1], preceding),
        )

    def grad_copies(j):
        return (
            remote(sent.at[j, 1], got.at[j, 0], gs_sem.at[j, 0], gr_sem.at[j, 0], following),
            remote(sent.at[j, 0], got.at[j, 1], gs_sem.at[j, 1], gr_sem.at[j, 1], preceding),
        )

    def out_own(j, a):
        return pltpu.make_async_copy(
            done.at[j, a, 0], outputs[a].at[:, :, mine + j], ol_sem.at[j, a]
        )

    def out_half(j, a):
        return remote(
            done.at[j, a, 1], outputs[a].at[:, :, mine + j], os_sem.at[j, a], or_sem.at[j, a], partner
        )

    def out_half_in(j, a):
        return remote(
            done.at[j, a, 1], outputs[a].at[:, :, theirs + j], os_sem.at[j, a], or_sem.at[j, a], partner
        )

    reach_copy = pltpu.make_async_copy(reach_in, reach, reach_sem)
    reach_copy.start()
    odd = tm % 2
    seam = (1 - odd) * flip_prev + odd * flip_next
    barrier = pltpu.get_barrier_semaphore()
    pl.semaphore_signal(barrier, inc=1, device_id=partner, device_id_type=MESH)

    @pl.when(odd == 1)
    def _():
        pl.semaphore_signal(barrier, inc=1, device_id=preceding, device_id_type=MESH)

    @pl.when((odd == 1) & (seam == 0))
    def _():
        pl.semaphore_signal(barrier, inc=1, device_id=following, device_id_type=MESH)

    @pl.when((odd == 0) & (seam == 1))
    def _():
        pl.semaphore_signal(barrier, inc=1, device_id=preceding, device_id_type=MESH)

    pl.semaphore_wait(barrier, 3 - 2 * odd + (2 * odd - 1) * seam)

    for first in (0, 2):

        def begin(j, carry, first=first):
            for a in (first, first + 1):
                half_copy(j, a).start()
            for a in (first, first + 1):
                own_copy(j, a).start()
            return carry

        lax.fori_loop(0, OWN, begin, 0)

    @pl.when(odd == 0)
    def _():
        pl.semaphore_signal(hello.at[0], inc=1, device_id=following, device_id_type=MESH)

    @pl.when((odd == 0) & (seam == 0))
    def _():
        pl.semaphore_signal(hello.at[1], inc=1, device_id=preceding, device_id_type=MESH)

    @pl.when((odd == 1) & (seam == 1))
    def _():
        pl.semaphore_signal(hello.at[1], inc=1, device_id=following, device_id_type=MESH)

    @pl.when(odd == 1)
    def _():
        pl.semaphore_wait(hello.at[0], 1)

    @pl.when(odd != seam)
    def _():
        pl.semaphore_wait(hello.at[1], 1)

    def flat(x):
        return x.reshape(TOKENS, SIZE)

    def tiled(x):
        return x.astype(jnp.bfloat16).reshape((2,) + HALF)

    def arrived(j, first):
        for a in (first, first + 1):
            own_copy(j, a).wait()
            half_copy(j, a).wait_recv()

    def forward(j, carry):
        arrived(j, 0)
        for copy in key_copies(j):
            copy.start()
        return carry

    lax.fori_loop(0, OWN, forward, 0)

    def compute(j, carry):
        arrived(j, 2)
        for copy in key_copies(j):
            copy.wait_recv()
        k, v, q, d = [flat(tile[j, a]) for a in range(4)]
        ks = [k, flat(near[j, 0, 0]), flat(near[j, 1, 0])]
        vs = [v, flat(near[j, 0, 1]), flat(near[j, 1, 1])]
        back = (reach[0, mine + j] >= 1) & (tm >= 1)
        ahead = (reach[1, mine + j] >= 1) & (tm < count - 1)
        biases = [None, jnp.where(back, 0.0, -1e30), jnp.where(ahead, 0.0, -1e30)]
        attended, grad_query, key_parts, value_parts = one_head(q, d, ks, vs, biases)
        for way in range(2):
            sent[j, way, 0] = tiled(key_parts[1 + way])
            sent[j, way, 1] = tiled(value_parts[1 + way])
        for copy in grad_copies(j):
            copy.start()
        done[j, 0] = tiled(attended)
        done[j, 1] = tiled(grad_query)
        for a in range(2):
            out_half(j, a).start()
            out_own(j, a).start()
        local_grad[j, 0] = key_parts[0]
        local_grad[j, 1] = value_parts[0]
        return carry

    reach_copy.wait()
    lax.fori_loop(0, OWN, compute, 0)

    def gather(j, carry):
        for copy in grad_copies(j):
            copy.wait_recv()
        for part in range(2):
            total = local_grad[j, part]
            for way in range(2):
                total = total + flat(got[j, way, part]).astype(jnp.float32)
            done[j, 2 + part] = tiled(total)
            out_half(j, 2 + part).start()
            out_own(j, 2 + part).start()
        return carry

    lax.fori_loop(0, OWN, gather, 0)

    def finish(j, carry):
        for a in range(4):
            half_copy(j, a).wait_send()
            out_own(j, a).wait()
            out_half(j, a).wait_send()
            out_half_in(j, a).wait_recv()
        for copy in key_copies(j) + grad_copies(j):
            copy.wait_send()
        return carry

    lax.fori_loop(0, OWN, finish, 0)


def deliver(*refs):
    got, outs, sem = refs[:4], refs[4:8], refs[8]
    copies = [pltpu.make_async_copy(g, o, sem.at[i]) for i, (g, o) in enumerate(zip(got, outs))]
    for copy in copies:
        copy.start()
    for copy in copies:
        copy.wait()


def local(queries, keys, values, grad_out, reach):
    def split(x):
        return x.reshape(FRAMES, ROWS, COLS, HEADS, SIZE).transpose(0, 2, 3, 1, 4)

    def join(x):
        return x.transpose(0, 3, 1, 2, 4).reshape(FRAMES, ROWS, COLS, HEADS * SIZE)

    shape = (FRAMES, COLS, HEADS, ROWS, SIZE)
    anywhere = pl.BlockSpec(memory_space=pl.ANY)
    sems = pltpu.SemaphoreType.DMA
    held = (reach, split(keys), split(values), split(queries), split(grad_out))
    outs = pl.pallas_call(
        kernel,
        out_shape=[jax.ShapeDtypeStruct(shape, jnp.bfloat16)] * 4,
        in_specs=[pl.BlockSpec(memory_space=pltpu.HBM)] * 5,
        out_specs=[anywhere] * 4,
        scratch_shapes=[
            pltpu.SMEM((2, HEADS), jnp.int32),
            pltpu.VMEM((OWN, 4, 2) + HALF, jnp.bfloat16),
            pltpu.VMEM((OWN, 2, 2, 2) + HALF, jnp.bfloat16),
            pltpu.VMEM((OWN, 2, TOKENS, SIZE), jnp.float32),
            pltpu.VMEM((OWN, 2, 2, 2) + HALF, jnp.bfloat16),
            pltpu.VMEM((OWN, 2, 2, 2) + HALF, jnp.bfloat16),
            pltpu.VMEM((OWN, 4, 2) + HALF, jnp.bfloat16),
            sems,
            sems((OWN, 4)), sems((OWN, 4)), sems((OWN, 4)),
            sems((OWN, 2)), sems((OWN, 2)), sems((OWN, 2)), sems((OWN, 2)),
            sems((OWN, 4)), sems((OWN, 4)), sems((OWN, 4)),
            pltpu.SemaphoreType.REGULAR((2,)),
        ],
        compiler_params=pltpu.CompilerParams(
            collective_id=0, has_side_effects=True, vmem_limit_bytes=24 << 20
        ),
    )(*[pltpu.with_memory_space_constraint(x, pltpu.HBM) for x in held])
    outs = pl.pallas_call(
        deliver,
        out_shape=[jax.ShapeDtypeStruct(shape, jnp.bfloat16)] * 4,
        in_specs=[anywhere] * 4,
        out_specs=[pl.BlockSpec(memory_space=pltpu.HBM)] * 4,
        scratch_shapes=[sems((4,))],
        compiler_params=pltpu.CompilerParams(vmem_limit_bytes=2 << 20),
    )(*outs)
    return tuple(join(x) for x in outs)


def solution(mesh):
    spec = P("tm", "height", None, None)
    return jax.shard_map(
        local,
        mesh=mesh,
        in_specs=(spec, spec, spec, spec, P()),
        out_specs=(spec, spec, spec, spec),
        check_vma=False,
    )
```

```python
import functools
import math

import jax
import jax.numpy as jnp
from jax import lax
from jax.experimental import pallas as pl
from jax.experimental.pallas import tpu as pltpu
from jax.sharding import PartitionSpec as P

MESH = pl.DeviceIdType.MESH
HEADS, SIZE = 12, 128
FRAMES, ROWS, COLS = 6, 4, 6
OWN = HEADS // 2
HALF = (FRAMES, COLS, ROWS, SIZE)
TOKENS = 2 * FRAMES * COLS * ROWS
FACTOR = SIZE**-0.5
FACTOR2 = FACTOR * math.log2(math.e)
RING = 32


def dot(a, b, over_a, over_b):
    return lax.dot_general(
        a, b, (((over_a,), (over_b,)), ((), ())), preferred_element_type=jnp.float32
    )


def one_head(q, d, ks, vs, biases):
    scores = [dot(q, k, 1, 1) for k in ks]
    scores = [s if b is None else s + b for s, b in zip(scores, biases)]
    top = functools.reduce(jnp.maximum, [jnp.max(s, axis=1, keepdims=True) for s in scores])
    raised = [jnp.exp2((s - top) * FACTOR2) for s in scores]
    total = sum(jnp.sum(e, axis=1, keepdims=True) for e in raised)
    inverse = 1.0 / total
    probability = [e * inverse for e in raised]
    weights = [p.astype(jnp.bfloat16) for p in probability]
    attended = sum(dot(w, v, 1, 0) for w, v in zip(weights, vs)).astype(jnp.bfloat16)
    row_dot = jnp.sum(
        attended.astype(jnp.float32) * d.astype(jnp.float32), axis=1, keepdims=True
    )
    grad_prob = [dot(d, v, 1, 1) for v in vs]
    grad_score = [
        (p * (g - row_dot)).astype(jnp.bfloat16) for p, g in zip(probability, grad_prob)
    ]
    grad_query = sum(dot(s, k, 1, 0) for s, k in zip(grad_score, ks)) * FACTOR
    key_parts = [dot(s, q, 0, 0) * FACTOR for s in grad_score]
    value_parts = [dot(w, d, 0, 0) for w in weights]
    return attended, grad_query.astype(jnp.bfloat16), key_parts, value_parts


def kernel(
    reach_in, k_in, v_in, q_in, d_in, o_out, dq_out, dk_out, dv_out,
    reach, tile, near, local_grad, sent, got, done, reach_sem,
    own_sem, xs_sem, xr_sem, ks_sem, kr_sem, gs_sem, gr_sem, os_sem, or_sem, ol_sem, hello,
):
    tm, height = lax.axis_index("tm"), lax.axis_index("height")
    count = lax.axis_size("tm")
    inputs = (k_in, v_in, q_in, d_in)
    outputs = (o_out, dq_out, dk_out, dv_out)
    other = height + 1 - 2 * (height % 2)
    partner = (tm, other)
    flip_next = (tm % RING + 1) // RING
    flip_prev = 1 - (tm % RING + RING - 1) // RING
    following = ((tm + 1) % count, height + flip_next * (other - height))
    preceding = ((tm + count - 1) % count, height + flip_prev * (other - height))
    side = (height % 2 + tm // RING) % 2
    mine, theirs = side * OWN, (1 - side) * OWN

    def own_copy(j, a):
        return pltpu.make_async_copy(
            inputs[a].at[:, :, mine + j], tile.at[j, a, 0], own_sem.at[a // 2]
        )

    def remote(src, dst, send, recv, device):
        return pltpu.make_async_remote_copy(
            src_ref=src, dst_ref=dst, send_sem=send, recv_sem=recv, device_id=device,
            device_id_type=MESH,
        )

    def half_copy(j, a):
        return remote(
            inputs[a].at[:, :, theirs + j], tile.at[j, a, 1], xs_sem, xr_sem.at[j, a // 2], partner
        )

    def key_copies(j):
        block = tile.at[j, pl.ds(0, 2)]
        return (
            remote(block, near.at[j, 0], ks_sem, kr_sem.at[j], following),
            remote(block, near.at[j, 1], ks_sem, kr_sem.at[j], preceding),
        )

    def grad_copies(j):
        return (
            remote(sent.at[j, 1], got.at[j, 0], gs_sem, gr_sem.at[j], following),
            remote(sent.at[j, 0], got.at[j, 1], gs_sem, gr_sem.at[j], preceding),
        )

    def out_own(j, a):
        return pltpu.make_async_copy(
            done.at[j, a, 0], outputs[a].at[:, :, mine + j], ol_sem
        )

    def out_half(j, a):
        return remote(
            done.at[j, a, 1], outputs[a].at[:, :, mine + j], os_sem, or_sem, partner
        )

    reach_copy = pltpu.make_async_copy(reach_in, reach, reach_sem)
    reach_copy.start()
    odd = tm % 2
    seam = (1 - odd) * flip_prev + odd * flip_next
    barrier = pltpu.get_barrier_semaphore()
    pl.semaphore_signal(barrier, inc=1, device_id=partner, device_id_type=MESH)

    @pl.when(odd == 1)
    def _():
        pl.semaphore_signal(barrier, inc=1, device_id=preceding, device_id_type=MESH)

    @pl.when((odd == 1) & (seam == 0))
    def _():
        pl.semaphore_signal(barrier, inc=1, device_id=following, device_id_type=MESH)

    @pl.when((odd == 0) & (seam == 1))
    def _():
        pl.semaphore_signal(barrier, inc=1, device_id=preceding, device_id_type=MESH)

    pl.semaphore_wait(barrier, 3 - 2 * odd + (2 * odd - 1) * seam)

    for first in (0, 2):

        def begin(j, carry, first=first):
            for a in (first, first + 1):
                half_copy(j, a).start()
            for a in (first, first + 1):
                own_copy(j, a).start()
            return carry

        lax.fori_loop(0, OWN, begin, 0)

    @pl.when(odd == 0)
    def _():
        pl.semaphore_signal(hello.at[0], inc=1, device_id=following, device_id_type=MESH)

    @pl.when((odd == 0) & (seam == 0))
    def _():
        pl.semaphore_signal(hello.at[1], inc=1, device_id=preceding, device_id_type=MESH)

    @pl.when((odd == 1) & (seam == 1))
    def _():
        pl.semaphore_signal(hello.at[1], inc=1, device_id=following, device_id_type=MESH)

    @pl.when(odd == 1)
    def _():
        pl.semaphore_wait(hello.at[0], 1)

    @pl.when(odd != seam)
    def _():
        pl.semaphore_wait(hello.at[1], 1)

    def flat(x):
        return x.reshape(TOKENS, SIZE)

    def tiled(x):
        return x.astype(jnp.bfloat16).reshape((2,) + HALF)

    def arrived(j, pair):
        halves = tile.at[j, pl.ds(2 * pair, 2)]
        remote(halves.at[:, 0], halves.at[:, 1], xs_sem, xr_sem.at[j, pair], partner).wait_recv()

    def own_arrived(pair):
        halves = tile.at[:, pl.ds(2 * pair, 2)]
        pltpu.make_async_copy(halves.at[:, :, 1], halves.at[:, :, 0], own_sem.at[pair]).wait()

    own_arrived(0)

    def forward(j, carry):
        arrived(j, 0)
        for copy in key_copies(j):
            copy.start()
        return carry

    lax.fori_loop(0, OWN, forward, 0)

    def compute(j, carry):
        arrived(j, 1)
        remote(sent.at[j], near.at[j], ks_sem, kr_sem.at[j], partner).wait_recv()
        k, v, q, d = [flat(tile[j, a]) for a in range(4)]
        ks = [k, flat(near[j, 0, 0]), flat(near[j, 1, 0])]
        vs = [v, flat(near[j, 0, 1]), flat(near[j, 1, 1])]
        back = (reach[0, mine + j] >= 1) & (tm >= 1)
        ahead = (reach[1, mine + j] >= 1) & (tm < count - 1)
        biases = [None, jnp.where(back, 0.0, -1e30), jnp.where(ahead, 0.0, -1e30)]
        attended, grad_query, key_parts, value_parts = one_head(q, d, ks, vs, biases)
        for way in range(2):
            sent[j, way, 0] = tiled(key_parts[1 + way])
            sent[j, way, 1] = tiled(value_parts[1 + way])
        for copy in grad_copies(j):
            copy.start()
        done[j, 0] = tiled(attended)
        done[j, 1] = tiled(grad_query)
        for a in range(2):
            out_half(j, a).start()
            out_own(j, a).start()
        local_grad[j, 0] = key_parts[0]
        local_grad[j, 1] = value_parts[0]
        return carry

    own_arrived(1)
    reach_copy.wait()
    lax.fori_loop(0, OWN, compute, 0)

    def gather(j, carry):
        remote(sent.at[j], got.at[j], gs_sem, gr_sem.at[j], partner).wait_recv()
        for part in range(2):
            total = local_grad[j, part]
            for way in range(2):
                total = total + flat(got[j, way, part]).astype(jnp.float32)
            done[j, 2 + part] = tiled(total)
            out_half(j, 2 + part).start()
            out_own(j, 2 + part).start()
        return carry

    lax.fori_loop(0, OWN, gather, 0)

    remote(tile.at[:, :, 0], tile.at[:, :, 1], xs_sem, xr_sem.at[0, 0], partner).wait_send()
    remote(near, got, ks_sem, kr_sem.at[0], partner).wait_send()
    remote(sent, got, gs_sem, gr_sem.at[0], partner).wait_send()
    pltpu.make_async_copy(done.at[:, :, 0], done.at[:, :, 1], ol_sem).wait()
    remote(done.at[:, :, 1], done.at[:, :, 0], os_sem, or_sem, partner).wait()


def deliver(*refs):
    got, outs, sem = refs[:4], refs[4:8], refs[8]
    copies = [pltpu.make_async_copy(g, o, sem.at[i]) for i, (g, o) in enumerate(zip(got, outs))]
    for copy in copies:
        copy.start()
    for copy in copies:
        copy.wait()


def local(queries, keys, values, grad_out, reach):
    def split(x):
        return x.reshape(FRAMES, ROWS, COLS, HEADS, SIZE).transpose(0, 2, 3, 1, 4)

    def join(x):
        return x.transpose(0, 3, 1, 2, 4).reshape(FRAMES, ROWS, COLS, HEADS * SIZE)

    shape = (FRAMES, COLS, HEADS, ROWS, SIZE)
    anywhere = pl.BlockSpec(memory_space=pl.ANY)
    sems = pltpu.SemaphoreType.DMA
    held = (reach, split(keys), split(values), split(queries), split(grad_out))
    outs = pl.pallas_call(
        kernel,
        out_shape=[jax.ShapeDtypeStruct(shape, jnp.bfloat16)] * 4,
        in_specs=[pl.BlockSpec(memory_space=pltpu.HBM)] * 5,
        out_specs=[anywhere] * 4,
        scratch_shapes=[
            pltpu.SMEM((2, HEADS), jnp.int32),
            pltpu.VMEM((OWN, 4, 2) + HALF, jnp.bfloat16),
            pltpu.VMEM((OWN, 2, 2, 2) + HALF, jnp.bfloat16),
            pltpu.VMEM((OWN, 2, TOKENS, SIZE), jnp.float32),
            pltpu.VMEM((OWN, 2, 2, 2) + HALF, jnp.bfloat16),
            pltpu.VMEM((OWN, 2, 2, 2) + HALF, jnp.bfloat16),
            pltpu.VMEM((OWN, 4, 2) + HALF, jnp.bfloat16),
            sems,
            sems((2,)), sems, sems((OWN, 2)),
            sems, sems((OWN,)), sems, sems((OWN,)),
            sems, sems, sems,
            pltpu.SemaphoreType.REGULAR((2,)),
        ],
        compiler_params=pltpu.CompilerParams(
            collective_id=0, has_side_effects=True, vmem_limit_bytes=24 << 20
        ),
    )(*[pltpu.with_memory_space_constraint(x, pltpu.HBM) for x in held])
    outs = pl.pallas_call(
        deliver,
        out_shape=[jax.ShapeDtypeStruct(shape, jnp.bfloat16)] * 4,
        in_specs=[anywhere] * 4,
        out_specs=[pl.BlockSpec(memory_space=pltpu.HBM)] * 4,
        scratch_shapes=[sems((4,))],
        compiler_params=pltpu.CompilerParams(vmem_limit_bytes=2 << 20),
    )(*outs)
    return tuple(join(x) for x in outs)


def solution(mesh):
    spec = P("tm", "height", None, None)
    return jax.shard_map(
        local,
        mesh=mesh,
        in_specs=(spec, spec, spec, spec, P()),
        out_specs=(spec, spec, spec, spec),
        check_vma=False,
    )
```

```python
import functools
import math

import jax
import jax.numpy as jnp
from jax import lax
from jax.experimental import pallas as pl
from jax.experimental.pallas import tpu as pltpu
from jax.sharding import PartitionSpec as P

MESH = pl.DeviceIdType.MESH
HEADS, SIZE = 12, 128
FRAMES, ROWS, COLS = 6, 4, 6
OWN = HEADS // 2
HALF = (FRAMES, COLS, ROWS, SIZE)
TOKENS = 2 * FRAMES * COLS * ROWS
FACTOR = SIZE**-0.5
FACTOR2 = FACTOR * math.log2(math.e)
RING = 32
EARLY = 4


def dot(a, b, over_a, over_b):
    return lax.dot_general(
        a, b, (((over_a,), (over_b,)), ((), ())), preferred_element_type=jnp.float32
    )


def one_head(q, d, ks, vs, biases):
    scores = [dot(q, k, 1, 1) for k in ks]
    scores = [s if b is None else s + b for s, b in zip(scores, biases)]
    top = functools.reduce(jnp.maximum, [jnp.max(s, axis=1, keepdims=True) for s in scores])
    raised = [jnp.exp2((s - top) * FACTOR2) for s in scores]
    total = sum(jnp.sum(e, axis=1, keepdims=True) for e in raised)
    inverse = 1.0 / total
    probability = [e * inverse for e in raised]
    weights = [p.astype(jnp.bfloat16) for p in probability]
    attended = sum(dot(w, v, 1, 0) for w, v in zip(weights, vs)).astype(jnp.bfloat16)
    row_dot = jnp.sum(
        attended.astype(jnp.float32) * d.astype(jnp.float32), axis=1, keepdims=True
    )
    grad_prob = [dot(d, v, 1, 1) for v in vs]
    grad_score = [
        (p * (g - row_dot)).astype(jnp.bfloat16) for p, g in zip(probability, grad_prob)
    ]
    grad_query = sum(dot(s, k, 1, 0) for s, k in zip(grad_score, ks)) * FACTOR
    key_parts = [dot(s, q, 0, 0) * FACTOR for s in grad_score]
    value_parts = [dot(w, d, 0, 0) for w in weights]
    return attended, grad_query.astype(jnp.bfloat16), key_parts, value_parts


def kernel(
    reach_in, k_in, v_in, q_in, d_in, o_out, dq_out, dk_out, dv_out,
    reach, tile, near, local_grad, sent, got, done, reach_sem,
    own_sem, xs_sem, xr_sem, ks_sem, kr_sem, gs_sem, gr_sem, os_sem, or_sem, ol_sem, hello,
):
    tm, height = lax.axis_index("tm"), lax.axis_index("height")
    count = lax.axis_size("tm")
    inputs = (k_in, v_in, q_in, d_in)
    outputs = (o_out, dq_out, dk_out, dv_out)
    other = height + 1 - 2 * (height % 2)
    partner = (tm, other)
    flip_next = (tm % RING + 1) // RING
    flip_prev = 1 - (tm % RING + RING - 1) // RING
    following = ((tm + 1) % count, height + flip_next * (other - height))
    preceding = ((tm + count - 1) % count, height + flip_prev * (other - height))
    side = (height % 2 + tm // RING) % 2
    mine, theirs = side * OWN, (1 - side) * OWN

    def own_copy(j, a):
        return pltpu.make_async_copy(
            inputs[a].at[:, :, mine + j], tile.at[j, a, 0], own_sem.at[a // 2]
        )

    def remote(src, dst, send, recv, device):
        return pltpu.make_async_remote_copy(
            src_ref=src, dst_ref=dst, send_sem=send, recv_sem=recv, device_id=device,
            device_id_type=MESH,
        )

    def half_copy(j, a):
        return remote(
            inputs[a].at[:, :, theirs + j], tile.at[j, a, 1], xs_sem, xr_sem.at[j // 2, a // 2], partner
        )

    def key_copies(j):
        block = tile.at[j, pl.ds(0, 2)]
        return (
            remote(block, near.at[j, 0], ks_sem, kr_sem.at[j // 2], following),
            remote(block, near.at[j, 1], ks_sem, kr_sem.at[j // 2], preceding),
        )

    def grad_copies(j):
        return (
            remote(sent.at[j, 1], got.at[j, 0], gs_sem, gr_sem.at[j // 2], following),
            remote(sent.at[j, 0], got.at[j, 1], gs_sem, gr_sem.at[j // 2], preceding),
        )

    def out_own(j, a):
        return pltpu.make_async_copy(
            done.at[j, a, 0], outputs[a].at[:, :, mine + j], ol_sem
        )

    def out_half(j, a, late=0):
        return remote(
            done.at[j, a, 1], outputs[a].at[:, :, mine + j], os_sem.at[late], or_sem, partner
        )

    barrier = pltpu.get_barrier_semaphore()
    pl.semaphore_signal(barrier, inc=1, device_id=partner, device_id_type=MESH)
    reach_copy = pltpu.make_async_copy(reach_in, reach, reach_sem)
    odd = tm % 2
    seam = (1 - odd) * flip_prev + odd * flip_next

    @pl.when(odd == 1)
    def _():
        pl.semaphore_signal(barrier, inc=1, device_id=preceding, device_id_type=MESH)

    @pl.when((odd == 1) & (seam == 0))
    def _():
        pl.semaphore_signal(barrier, inc=1, device_id=following, device_id_type=MESH)

    @pl.when((odd == 0) & (seam == 1))
    def _():
        pl.semaphore_signal(barrier, inc=1, device_id=preceding, device_id_type=MESH)

    pl.semaphore_wait(barrier, 3 - 2 * odd + (2 * odd - 1) * seam)

    for first in (0, 2):

        def begin(j, carry, first=first):
            for a in (first, first + 1):
                half_copy(j, a).start()
            for a in (first, first + 1):
                own_copy(j, a).start()
            return carry

        lax.fori_loop(0, OWN, begin, 0)

    reach_copy.start()

    @pl.when(odd == 0)
    def _():
        pl.semaphore_signal(hello.at[0], inc=1, device_id=following, device_id_type=MESH)

    @pl.when((odd == 0) & (seam == 0))
    def _():
        pl.semaphore_signal(hello.at[1], inc=1, device_id=preceding, device_id_type=MESH)

    @pl.when((odd == 1) & (seam == 1))
    def _():
        pl.semaphore_signal(hello.at[1], inc=1, device_id=following, device_id_type=MESH)

    @pl.when(odd == 1)
    def _():
        pl.semaphore_wait(hello.at[0], 1)

    @pl.when(odd != seam)
    def _():
        pl.semaphore_wait(hello.at[1], 1)

    def flat(x):
        return x.reshape(TOKENS, SIZE)

    def tiled(x):
        return x.astype(jnp.bfloat16).reshape((2,) + HALF)

    def arrived(j, pair):
        @pl.when(j % 2 == 0)
        def _():
            halves = tile.at[pl.ds(j, 2), pl.ds(2 * pair, 2)]
            remote(
                halves.at[:, :, 0], halves.at[:, :, 1], xs_sem, xr_sem.at[j // 2, pair], partner
            ).wait_recv()

    def own_arrived(pair):
        halves = tile.at[:, pl.ds(2 * pair, 2)]
        pltpu.make_async_copy(halves.at[:, :, 1], halves.at[:, :, 0], own_sem.at[pair]).wait()

    own_arrived(0)

    def forward(j, carry):
        arrived(j, 0)
        for copy in key_copies(j):
            copy.start()
        return carry

    lax.fori_loop(0, OWN, forward, 0)

    def compute(j, carry):
        arrived(j, 1)

        @pl.when(j % 2 == 0)
        def _():
            two = pl.ds(j, 2)
            remote(sent.at[two], near.at[two], ks_sem, kr_sem.at[j // 2], partner).wait_recv()

        k, v, q, d = [flat(tile[j, a]) for a in range(4)]
        ks = [k, flat(near[j, 0, 0]), flat(near[j, 1, 0])]
        vs = [v, flat(near[j, 0, 1]), flat(near[j, 1, 1])]
        back = (reach[0, mine + j] >= 1) & (tm >= 1)
        ahead = (reach[1, mine + j] >= 1) & (tm < count - 1)
        biases = [None, jnp.where(back, 0.0, -1e30), jnp.where(ahead, 0.0, -1e30)]
        attended, grad_query, key_parts, value_parts = one_head(q, d, ks, vs, biases)
        for way in range(2):
            sent[j, way, 0] = tiled(key_parts[1 + way])
            sent[j, way, 1] = tiled(value_parts[1 + way])
        for copy in grad_copies(j):
            copy.start()
        done[j, 0] = tiled(attended)
        done[j, 1] = tiled(grad_query)
        for a in range(2):
            out_half(j, a).start()
            out_own(j, a).start()
        local_grad[j, 0] = key_parts[0]
        local_grad[j, 1] = value_parts[0]
        return carry

    own_arrived(1)
    reach_copy.wait()
    lax.fori_loop(0, OWN, compute, 0)

    def early_left():
        first = done.at[pl.ds(0, EARLY), pl.ds(2, 2)]
        remote(first.at[:, :, 0], first.at[:, :, 1], os_sem.at[1], or_sem, partner).wait_send()

    def gather(j, carry):
        late = 1 + j // EARLY

        @pl.when((j == EARLY) & (odd == 1))
        def _():
            early_left()

        @pl.when(j % 2 == 0)
        def _():
            two = pl.ds(j, 2)
            remote(sent.at[two], got.at[two], gs_sem, gr_sem.at[j // 2], partner).wait_recv()

        for part in range(2):
            total = local_grad[j, part]
            for way in range(2):
                total = total + flat(got[j, way, part]).astype(jnp.float32)
            done[j, 2 + part] = tiled(total)
            out_half(j, 2 + part, late).start()
            out_own(j, 2 + part).start()
        return carry

    lax.fori_loop(0, OWN, gather, 0)

    remote(tile.at[:, :, 0], tile.at[:, :, 1], xs_sem, xr_sem.at[0, 0], partner).wait_send()
    remote(near, got, ks_sem, kr_sem.at[0], partner).wait_send()
    remote(sent, got, gs_sem, gr_sem.at[0], partner).wait_send()
    pltpu.make_async_copy(done.at[:, :, 0], done.at[:, :, 1], ol_sem).wait()

    @pl.when(odd == 0)
    def _():
        early_left()

    both = done.at[:, pl.ds(0, 2)]
    last = done.at[pl.ds(EARLY, OWN - EARLY), pl.ds(2, 2)]
    remote(both.at[:, :, 0], both.at[:, :, 1], os_sem.at[0], or_sem, partner).wait_send()
    remote(last.at[:, :, 0], last.at[:, :, 1], os_sem.at[2], or_sem, partner).wait_send()
    remote(done.at[:, :, 1], done.at[:, :, 0], os_sem.at[0], or_sem, partner).wait_recv()


def deliver(*refs):
    got, outs, sem = refs[:4], refs[4:8], refs[8]
    copies = [pltpu.make_async_copy(g, o, sem.at[i]) for i, (g, o) in enumerate(zip(got, outs))]
    for copy in copies:
        copy.start()
    for copy in copies:
        copy.wait()


def local(queries, keys, values, grad_out, reach):
    def split(x):
        return x.reshape(FRAMES, ROWS, COLS, HEADS, SIZE).transpose(0, 2, 3, 1, 4)

    def join(x):
        return x.transpose(0, 3, 1, 2, 4).reshape(FRAMES, ROWS, COLS, HEADS * SIZE)

    shape = (FRAMES, COLS, HEADS, ROWS, SIZE)
    anywhere = pl.BlockSpec(memory_space=pl.ANY)
    sems = pltpu.SemaphoreType.DMA
    held = (reach, split(keys), split(values), split(queries), split(grad_out))
    outs = pl.pallas_call(
        kernel,
        out_shape=[jax.ShapeDtypeStruct(shape, jnp.bfloat16)] * 4,
        in_specs=[pl.BlockSpec(memory_space=pltpu.HBM)] * 5,
        out_specs=[anywhere] * 4,
        scratch_shapes=[
            pltpu.SMEM((2, HEADS), jnp.int32),
            pltpu.VMEM((OWN, 4, 2) + HALF, jnp.bfloat16),
            pltpu.VMEM((OWN, 2, 2, 2) + HALF, jnp.bfloat16),
            pltpu.VMEM((OWN, 2, TOKENS, SIZE), jnp.float32),
            pltpu.VMEM((OWN, 2, 2, 2) + HALF, jnp.bfloat16),
            pltpu.VMEM((OWN, 2, 2, 2) + HALF, jnp.bfloat16),
            pltpu.VMEM((OWN, 4, 2) + HALF, jnp.bfloat16),
            sems,
            sems((2,)), sems, sems((OWN // 2, 2)),
            sems, sems((OWN // 2,)), sems, sems((OWN // 2,)),
            sems((3,)), sems, sems,
            pltpu.SemaphoreType.REGULAR((2,)),
        ],
        compiler_params=pltpu.CompilerParams(
            collective_id=0, has_side_effects=True, vmem_limit_bytes=24 << 20
        ),
    )(*[pltpu.with_memory_space_constraint(x, pltpu.HBM) for x in held])
    outs = pl.pallas_call(
        deliver,
        out_shape=[jax.ShapeDtypeStruct(shape, jnp.bfloat16)] * 4,
        in_specs=[anywhere] * 4,
        out_specs=[pl.BlockSpec(memory_space=pltpu.HBM)] * 4,
        scratch_shapes=[sems((4,))],
        compiler_params=pltpu.CompilerParams(vmem_limit_bytes=2 << 20),
    )(*outs)
    return tuple(join(x) for x in outs)


def solution(mesh):
    spec = P("tm", "height", None, None)
    return jax.shard_map(
        local,
        mesh=mesh,
        in_specs=(spec, spec, spec, spec, P()),
        out_specs=(spec, spec, spec, spec),
        check_vma=False,
    )
```

```python
import functools
import math

import jax
import jax.numpy as jnp
from jax import lax
from jax.experimental import pallas as pl
from jax.experimental.pallas import tpu as pltpu
from jax.sharding import PartitionSpec as P

MESH = pl.DeviceIdType.MESH
HEADS, SIZE = 12, 128
FRAMES, ROWS, COLS = 6, 4, 6
OWN = HEADS // 2
HALF = (FRAMES, COLS, ROWS, SIZE)
TOKENS = 2 * FRAMES * COLS * ROWS
FACTOR = SIZE**-0.5
FACTOR2 = FACTOR * math.log2(math.e)
RING = 32
EARLY = 4


def dot(a, b, over_a, over_b):
    return lax.dot_general(
        a, b, (((over_a,), (over_b,)), ((), ())), preferred_element_type=jnp.float32
    )


def one_head(q, d, ks, vs, biases):
    scores = [dot(q, k, 1, 1) for k in ks]
    scores = [s if b is None else s + b for s, b in zip(scores, biases)]
    top = functools.reduce(jnp.maximum, [jnp.max(s, axis=1, keepdims=True) for s in scores])
    raised = [jnp.exp2((s - top) * FACTOR2) for s in scores]
    total = sum(jnp.sum(e, axis=1, keepdims=True) for e in raised)
    inverse = 1.0 / total
    probability = [e * inverse for e in raised]
    weights = [p.astype(jnp.bfloat16) for p in probability]
    attended = sum(dot(w, v, 1, 0) for w, v in zip(weights, vs)).astype(jnp.bfloat16)
    row_dot = jnp.sum(
        attended.astype(jnp.float32) * d.astype(jnp.float32), axis=1, keepdims=True
    )
    grad_prob = [dot(d, v, 1, 1) for v in vs]
    grad_score = [
        (p * (g - row_dot)).astype(jnp.bfloat16) for p, g in zip(probability, grad_prob)
    ]
    grad_query = sum(dot(s, k, 1, 0) for s, k in zip(grad_score, ks)) * FACTOR
    key_parts = [dot(s, q, 0, 0) * FACTOR for s in grad_score]
    value_parts = [dot(w, d, 0, 0) for w in weights]
    return attended, grad_query.astype(jnp.bfloat16), key_parts, value_parts


def kernel(
    reach_in, k_in, v_in, q_in, d_in, o_out, dq_out, dk_out, dv_out,
    reach, tile, near, local_grad, sent, got, done, reach_sem,
    own_sem, xs_sem, xr_sem, ks_sem, kr_sem, gs_sem, gr_sem, os_sem, or_sem, ol_sem, hello,
):
    tm, height = lax.axis_index("tm"), lax.axis_index("height")
    count = lax.axis_size("tm")
    inputs = (k_in, v_in, q_in, d_in)
    outputs = (o_out, dq_out, dk_out, dv_out)
    other = height + 1 - 2 * (height % 2)
    partner = (tm, other)
    flip_next = (tm % RING + 1) // RING
    flip_prev = 1 - (tm % RING + RING - 1) // RING
    following = ((tm + 1) % count, height + flip_next * (other - height))
    preceding = ((tm + count - 1) % count, height + flip_prev * (other - height))
    side = (height % 2 + tm // RING) % 2
    mine, theirs = side * OWN, (1 - side) * OWN

    def own_copy(j, a):
        return pltpu.make_async_copy(
            inputs[a].at[:, :, mine + j], tile.at[j, a, 0], own_sem.at[a // 2]
        )

    def remote(src, dst, send, recv, device):
        return pltpu.make_async_remote_copy(
            src_ref=src, dst_ref=dst, send_sem=send, recv_sem=recv, device_id=device,
            device_id_type=MESH,
        )

    def half_copy(j, a):
        return remote(
            inputs[a].at[:, :, theirs + j], tile.at[j, a, 1], xs_sem, xr_sem.at[j, a // 2], partner
        )

    def key_copies(j):
        block = tile.at[j, pl.ds(0, 2)]
        return (
            remote(block, near.at[j, 0], ks_sem, kr_sem.at[j], following),
            remote(block, near.at[j, 1], ks_sem, kr_sem.at[j], preceding),
        )

    def grad_copies(j):
        return (
            remote(sent.at[j, 1], got.at[j, 0], gs_sem, gr_sem.at[j], following),
            remote(sent.at[j, 0], got.at[j, 1], gs_sem, gr_sem.at[j], preceding),
        )

    def out_own(j, a):
        return pltpu.make_async_copy(
            done.at[j, a, 0], outputs[a].at[:, :, mine + j], ol_sem
        )

    def out_half(j, a, late=0):
        return remote(
            done.at[j, a, 1], outputs[a].at[:, :, mine + j], os_sem.at[late], or_sem, partner
        )

    barrier = pltpu.get_barrier_semaphore()
    pl.semaphore_signal(barrier, inc=1, device_id=partner, device_id_type=MESH)
    reach_copy = pltpu.make_async_copy(reach_in, reach, reach_sem)
    odd = tm % 2
    seam = (1 - odd) * flip_prev + odd * flip_next

    @pl.when(odd == 1)
    def _():
        pl.semaphore_signal(barrier, inc=1, device_id=preceding, device_id_type=MESH)

    @pl.when((odd == 1) & (seam == 0))
    def _():
        pl.semaphore_signal(barrier, inc=1, device_id=following, device_id_type=MESH)

    @pl.when((odd == 0) & (seam == 1))
    def _():
        pl.semaphore_signal(barrier, inc=1, device_id=preceding, device_id_type=MESH)

    pl.semaphore_wait(barrier, 3 - 2 * odd + (2 * odd - 1) * seam)

    for first in (0, 2):

        def begin(j, carry, first=first):
            for a in (first, first + 1):
                half_copy(j, a).start()
            for a in (first, first + 1):
                own_copy(j, a).start()
            return carry

        lax.fori_loop(0, OWN, begin, 0)

    reach_copy.start()

    @pl.when(odd == 0)
    def _():
        pl.semaphore_signal(hello.at[0], inc=1, device_id=following, device_id_type=MESH)

    @pl.when((odd == 0) & (seam == 0))
    def _():
        pl.semaphore_signal(hello.at[1], inc=1, device_id=preceding, device_id_type=MESH)

    @pl.when((odd == 1) & (seam == 1))
    def _():
        pl.semaphore_signal(hello.at[1], inc=1, device_id=following, device_id_type=MESH)

    @pl.when(odd == 1)
    def _():
        pl.semaphore_wait(hello.at[0], 1)

    @pl.when(odd != seam)
    def _():
        pl.semaphore_wait(hello.at[1], 1)

    def flat(x):
        return x.reshape(TOKENS, SIZE)

    def tiled(x):
        return x.astype(jnp.bfloat16).reshape((2,) + HALF)

    def arrived(j, pair):
        halves = tile.at[j, pl.ds(2 * pair, 2)]
        remote(halves.at[:, 0], halves.at[:, 1], xs_sem, xr_sem.at[j, pair], partner).wait_recv()

    def own_arrived(pair):
        halves = tile.at[:, pl.ds(2 * pair, 2)]
        pltpu.make_async_copy(halves.at[:, :, 1], halves.at[:, :, 0], own_sem.at[pair]).wait()

    own_arrived(0)

    def forward(j, carry):
        arrived(j, 0)
        for copy in key_copies(j):
            copy.start()
        return carry

    lax.fori_loop(0, OWN, forward, 0)

    def compute(j, carry):
        arrived(j, 1)
        remote(sent.at[j], near.at[j], ks_sem, kr_sem.at[j], partner).wait_recv()
        k, v, q, d = [flat(tile[j, a]) for a in range(4)]
        ks = [k, flat(near[j, 0, 0]), flat(near[j, 1, 0])]
        vs = [v, flat(near[j, 0, 1]), flat(near[j, 1, 1])]
        back = (reach[0, mine + j] >= 1) & (tm >= 1)
        ahead = (reach[1, mine + j] >= 1) & (tm < count - 1)
        biases = [None, jnp.where(back, 0.0, -1e30), jnp.where(ahead, 0.0, -1e30)]
        attended, grad_query, key_parts, value_parts = one_head(q, d, ks, vs, biases)
        for way in range(2):
            sent[j, way, 0] = tiled(key_parts[1 + way])
            sent[j, way, 1] = tiled(value_parts[1 + way])
        for copy in grad_copies(j):
            copy.start()
        done[j, 0] = tiled(attended)
        done[j, 1] = tiled(grad_query)
        for a in range(2):
            out_half(j, a).start()
            out_own(j, a).start()
        local_grad[j, 0] = key_parts[0]
        local_grad[j, 1] = value_parts[0]
        return carry

    own_arrived(1)
    reach_copy.wait()
    lax.fori_loop(0, OWN, compute, 0)

    def early_left():
        first = done.at[pl.ds(0, EARLY), pl.ds(2, 2)]
        remote(first.at[:, :, 0], first.at[:, :, 1], os_sem.at[1], or_sem, partner).wait_send()

    def gather(j, carry):
        late = 1 + j // EARLY

        @pl.when((j == EARLY) & (odd == 1))
        def _():
            early_left()

        remote(sent.at[j], got.at[j], gs_sem, gr_sem.at[j], partner).wait_recv()
        for part in range(2):
            total = local_grad[j, part]
            for way in range(2):
                total = total + flat(got[j, way, part]).astype(jnp.float32)
            done[j, 2 + part] = tiled(total)
            out_half(j, 2 + part, late).start()
            out_own(j, 2 + part).start()
        return carry

    lax.fori_loop(0, OWN, gather, 0)

    remote(tile.at[:, :, 0], tile.at[:, :, 1], xs_sem, xr_sem.at[0, 0], partner).wait_send()
    remote(near, got, ks_sem, kr_sem.at[0], partner).wait_send()
    remote(sent, got, gs_sem, gr_sem.at[0], partner).wait_send()
    pltpu.make_async_copy(done.at[:, :, 0], done.at[:, :, 1], ol_sem).wait()

    @pl.when(odd == 0)
    def _():
        early_left()

    both = done.at[:, pl.ds(0, 2)]
    last = done.at[pl.ds(EARLY, OWN - EARLY), pl.ds(2, 2)]
    remote(both.at[:, :, 0], both.at[:, :, 1], os_sem.at[0], or_sem, partner).wait_send()
    remote(last.at[:, :, 0], last.at[:, :, 1], os_sem.at[2], or_sem, partner).wait_send()
    remote(done.at[:, :, 1], done.at[:, :, 0], os_sem.at[0], or_sem, partner).wait_recv()


def deliver(*refs):
    got, outs, sem = refs[:4], refs[4:8], refs[8]
    copies = [pltpu.make_async_copy(g, o, sem.at[i]) for i, (g, o) in enumerate(zip(got, outs))]
    for copy in copies:
        copy.start()
    for copy in copies:
        copy.wait()


def local(queries, keys, values, grad_out, reach):
    def split(x):
        return x.reshape(FRAMES, ROWS, COLS, HEADS, SIZE).transpose(0, 2, 3, 1, 4)

    def join(x):
        return x.transpose(0, 3, 1, 2, 4).reshape(FRAMES, ROWS, COLS, HEADS * SIZE)

    shape = (FRAMES, COLS, HEADS, ROWS, SIZE)
    anywhere = pl.BlockSpec(memory_space=pl.ANY)
    sems = pltpu.SemaphoreType.DMA
    held = (reach, split(keys), split(values), split(queries), split(grad_out))
    outs = pl.pallas_call(
        kernel,
        out_shape=[jax.ShapeDtypeStruct(shape, jnp.bfloat16)] * 4,
        in_specs=[pl.BlockSpec(memory_space=pltpu.HBM)] * 5,
        out_specs=[anywhere] * 4,
        scratch_shapes=[
            pltpu.SMEM((2, HEADS), jnp.int32),
            pltpu.VMEM((OWN, 4, 2) + HALF, jnp.bfloat16),
            pltpu.VMEM((OWN, 2, 2, 2) + HALF, jnp.bfloat16),
            pltpu.VMEM((OWN, 2, TOKENS, SIZE), jnp.float32),
            pltpu.VMEM((OWN, 2, 2, 2) + HALF, jnp.bfloat16),
            pltpu.VMEM((OWN, 2, 2, 2) + HALF, jnp.bfloat16),
            pltpu.VMEM((OWN, 4, 2) + HALF, jnp.bfloat16),
            sems,
            sems((2,)), sems, sems((OWN, 2)),
            sems, sems((OWN,)), sems, sems((OWN,)),
            sems((3,)), sems, sems,
            pltpu.SemaphoreType.REGULAR((2,)),
        ],
        compiler_params=pltpu.CompilerParams(
            collective_id=0, has_side_effects=True, vmem_limit_bytes=24 << 20
        ),
    )(*[pltpu.with_memory_space_constraint(x, pltpu.HBM) for x in held])
    outs = pl.pallas_call(
        deliver,
        out_shape=[jax.ShapeDtypeStruct(shape, jnp.bfloat16)] * 4,
        in_specs=[anywhere] * 4,
        out_specs=[pl.BlockSpec(memory_space=pltpu.HBM)] * 4,
        scratch_shapes=[sems((4,))],
        compiler_params=pltpu.CompilerParams(vmem_limit_bytes=2 << 20),
    )(*outs)
    return tuple(join(x) for x in outs)


def solution(mesh):
    spec = P("tm", "height", None, None)
    return jax.shard_map(
        local,
        mesh=mesh,
        in_specs=(spec, spec, spec, spec, P()),
        out_specs=(spec, spec, spec, spec),
        check_vma=False,
    )
```
